256 devices in a mesh: row: 32 (over z_hi, x, core), col: 8 (over z_lo, y).
Axes of the slice: x: 4, y: 4, z: 8 (z_hi: 4, z_lo: 2; z = z_hi * 2 + z_lo), core: 2. Of those that a mesh axis runs over, the one named last changes fastest.
Arguments:
- planes: bfloat16 [4, 448, 896], P(None, 'row', 'col'), may hold values from -6 to 6
- pattern: int32 [1], replicated, may hold values from 0 to 3
- candidate: int32 [5], replicated, may hold values from 0 to 3
- stem_bank: bfloat16 [4, 9, 64, 4], replicated, may hold values from -1 to 1
- layer_bank: bfloat16 [4, 4, 9, 64, 64], replicated, may hold values from -0.25 to 0.25
- embed_weight: bfloat16 [64, 128], replicated, may hold values from -0.75 to 0.75
- norm_gains: float32 [5, 128], replicated, may hold values from 0.1 to 1.9
- qkv_weight: bfloat16 [2, 128, 384], replicated, may hold values from -4 to 4, as said below
- proj_weight: bfloat16 [2, 128, 128], replicated, may hold values from -0.5 to 0.5
- rel_table: float32 [2, 4, 169], replicated, may hold values from -4 to 4
- fc1_weight: bfloat16 [2, 128, 512], replicated, may hold values from -0.5 to 0.5
- fc2_weight: bfloat16 [2, 512, 128], replicated, may hold values from -0.25 to 0.25
- labels: int32 [448, 896], P('row', 'col'), may hold values from 1 to 4
Outputs:
- features: bfloat16 [448, 896, 128], P('row', 'col')
The draws below stay inside these ranges and needn't reach their ends.
Inputs may be any that keep to these rules, and one draw needn't show every extreme that they name: `pattern`: 0 RGGB, 1 GRBG, 2 GBRG, 3 BGGR. `labels`: sites attend only to sites of the same label. `qkv_weight`: entries of mean 0, of scale about 1 / sqrt(128) on the values.
All inputs are finite; a program needn't handle non-finite values.
Results may differ from the reference program's by a relative error of at most 0.025.
Values may be sent and summed in bfloat16 or wider, within the bound.
No kernel may reach another device: no remote copies, remote signals or barrier semaphores. Data moves between devices by JAX's collectives and lax.ppermute only.
A program may use at most 128 MiB of HBM per device.

```python
import jax
import jax.numpy as jnp
import numpy as np
from jax import lax

C = 64
D = 128
HEADS = 4
HD = 32
MLP = 512
WIN = 7
LAYERS = 5
NOPT = 4
ROWS = 448
COLS = 896


def draw_qkv_weight(key, part):
    key = jax.random.fold_in(key, 11)
    base_key = jax.random.fold_in(key, 1)
    weights = jax.random.normal(base_key, (2, D, 3 * D), jnp.float32) * D ** (-0.5)
    return jnp.clip(weights, -4.0, 4.0).astype(jnp.bfloat16)


def with_ends(entries, stream_key, smallest, largest):
    longest = entries.shape.index(max(entries.shape))
    spots = []
    for shift in (0, 1):
        where = [jax.random.randint(jax.random.fold_in(stream_key, axis), (), 0, length) for axis, length in enumerate(entries.shape)]
        where[longest] = (where[longest] + shift) % entries.shape[longest]
        spots.append(tuple(where))
    return entries.at[spots[0]].set(smallest).at[spots[1]].set(largest)


def block_scale(own_key, dims, cuts, least, high):
    level, own = 1.0, jax.random.fold_in(own_key, 6)
    for axis_at, shards_of in cuts:
        heights = jnp.exp(jax.random.uniform(jax.random.fold_in(own, axis_at), (shards_of,), jnp.float32, least / len(cuts), high / len(cuts)))
        level = level * jnp.repeat(heights, dims[axis_at] // shards_of).reshape([-1 if axis == axis_at else 1 for axis in range(len(dims))])
    return level


def gaussian(stream_key, extent, width, most, cuts=(), kind=jnp.bfloat16):
    loudness = block_scale(stream_key, extent, cuts, -0.22, 0.18) if cuts else 1.0
    values = jax.random.normal(stream_key, extent, jnp.float32) * width * loudness
    return jnp.minimum(jnp.maximum(values, -most), most).astype(kind)


def setup_inputs(seed: int = 0) -> dict:
    streams_of = jax.random.split(jax.random.key(seed), 14)
    return {
        "planes": gaussian(streams_of[0], (4, ROWS, COLS), 1.0, 6.0, ((1, 32), (2, 8))),
        "pattern": jax.random.randint(streams_of[1], (1,), 0, 4).astype(jnp.int32),
        "candidate": with_ends(jax.random.randint(streams_of[2], (LAYERS,), 0, NOPT), jax.random.fold_in(streams_of[2], 1), 0, NOPT - 1).astype(jnp.int32),
        "stem_bank": gaussian(streams_of[3], (NOPT, 9, C, 4), 36 ** -0.5, 1.0),
        "layer_bank": gaussian(streams_of[4], (LAYERS - 1, NOPT, 9, C, C), (9 * C) ** -0.5, 0.25),
        "embed_weight": gaussian(streams_of[5], (C, D), C ** -0.5, 0.75),
        "norm_gains": jnp.clip(1.0 + 0.18 * jax.random.normal(streams_of[6], (5, D), jnp.float32), 0.1, 1.9),
        "qkv_weight": draw_qkv_weight(jax.random.fold_in(streams_of[13], 71), 0),
        "proj_weight": gaussian(streams_of[8], (2, D, D), D ** -0.5, 0.5),
        "rel_table": gaussian(streams_of[9], (2, HEADS, (2 * WIN - 1) * (2 * WIN - 1)), 1.0, 4.0, (), jnp.float32),
        "fc1_weight": gaussian(streams_of[10], (2, D, MLP), D ** -0.5, 0.5),
        "fc2_weight": gaussian(streams_of[11], (2, MLP, D), MLP ** -0.5, 0.25),
        "labels": with_ends(jax.random.randint(streams_of[12], (ROWS, COLS), 1, 5), jax.random.fold_in(streams_of[12], 1), 1, 4).astype(jnp.int32),
    }


ORDERS = np.array([[0, 1, 2, 3], [1, 0, 3, 2], [2, 0, 3, 1], [3, 1, 2, 0]], np.int32)
EPSILON = 1e-05

def offsets_table(window):
    across = np.arange(window * window) // window
    along = np.arange(window * window) % window
    return ((across[:, None] - across[None, :] + window - 1) * (2 * window - 1) + (along[:, None] - along[None, :] + window - 1)).astype(np.int32)

def conv_valid(source, kernels):
    height = source.shape[1] - 2
    breadth = source.shape[2] - 2
    summed = jnp.zeros((kernels.shape[1], height, breadth), jnp.float32)
    for offset in range(9):
        row_off = offset // 3
        col_off = offset % 3
        section = source[:, row_off:row_off + height, col_off:col_off + breadth].astype(jnp.float32)
        summed = summed + jnp.einsum('oc,chw->ohw', kernels[offset].astype(jnp.float32), section)
    return summed

def layer_norm(values, scales):
    centre = lax.optimization_barrier(jnp.mean(values, -1, keepdims=True))
    centred = values - centre
    spread = lax.optimization_barrier(jnp.mean(centred * centred, -1, keepdims=True))
    return centred * lax.rsqrt(spread + EPSILON) * scales

def to_windows(values, wrows, wcols):
    trailing = values.shape[2:]
    return values.reshape((wrows, WIN, wcols, WIN) + trailing).swapaxes(1, 2).reshape((wrows * wcols, WIN * WIN) + trailing)

def from_windows(blocks, wrows, wcols):
    trailing = blocks.shape[2:]
    return blocks.reshape((wrows, wcols, WIN, WIN) + trailing).swapaxes(1, 2).reshape((wrows * WIN, wcols * WIN) + trailing)

def attend(tokens, regions, scales, qkv, projection, table):
    count = tokens.shape[0]
    normed = layer_norm(tokens.astype(jnp.float32), scales).astype(jnp.bfloat16)
    triple = jnp.einsum('ntd,de->nte', normed.astype(jnp.float32), qkv.astype(jnp.float32)).astype(jnp.bfloat16)
    queries = triple[:, :, :D].reshape(count, WIN * WIN, HEADS, HD).astype(jnp.float32)
    keyset = triple[:, :, D:2 * D].reshape(count, WIN * WIN, HEADS, HD).astype(jnp.float32)
    valueset = triple[:, :, 2 * D:].reshape(count, WIN * WIN, HEADS, HD).astype(jnp.float32)
    offsets = jnp.asarray(offsets_table(WIN))
    scores = jnp.einsum('nihc,njhc->nhij', queries, keyset) * HD ** (-0.5) + table[:, offsets][None]
    allowed = regions[:, None, :, None] == regions[:, None, None, :]
    scores = jnp.where(allowed, scores, -jnp.inf)
    summit = lax.optimization_barrier(jnp.max(scores, -1, keepdims=True))
    weights = jnp.exp(scores - summit)
    probs = (weights / lax.optimization_barrier(jnp.sum(weights, -1, keepdims=True))).astype(jnp.bfloat16)
    mixed = jnp.einsum('nhij,njhc->nihc', probs.astype(jnp.float32), valueset).astype(jnp.bfloat16)
    mixed = mixed.reshape(count, WIN * WIN, D)
    return tokens.astype(jnp.float32) + jnp.einsum('ntd,de->nte', mixed.astype(jnp.float32), projection.astype(jnp.float32))

def feedforward(hidden, scales, first, second):
    normed = layer_norm(hidden, scales).astype(jnp.bfloat16)
    inner = jnp.einsum('hwd,de->hwe', normed.astype(jnp.float32), first.astype(jnp.float32))
    inner = jax.nn.gelu(inner, approximate=False).astype(jnp.bfloat16)
    return (hidden + jnp.einsum('hwd,de->hwe', inner.astype(jnp.float32), second.astype(jnp.float32))).astype(jnp.bfloat16)

def reference(planes, pattern, candidate, stem_bank, layer_bank, embed_weight, norm_gains, qkv_weight, proj_weight, rel_table, fc1_weight, fc2_weight, labels):
    ordering = jnp.asarray(ORDERS)[pattern[0]]
    canonical = jnp.take(planes, ordering, axis=0)
    pad_spec = ((0, 0), (1, 1), (1, 1))
    current = conv_valid(jnp.pad(canonical, pad_spec), stem_bank[candidate[0]]).astype(jnp.bfloat16)
    for layer in range(1, LAYERS):
        active = jax.nn.silu(current.astype(jnp.float32)).astype(jnp.bfloat16)
        update = conv_valid(jnp.pad(active, pad_spec), layer_bank[layer - 1][candidate[layer]])
        current = (current.astype(jnp.float32) + update).astype(jnp.bfloat16)
    embedded = jnp.einsum('chw,cd->hwd', current.astype(jnp.float32), embed_weight.astype(jnp.float32))
    first_in = layer_norm(embedded, norm_gains[0]).astype(jnp.bfloat16)
    strip_rows = ROWS // WIN
    plain_cols = COLS // WIN

    def plain_strip(pieces):
        strip, strip_labels = pieces
        blocks = to_windows(strip, 1, plain_cols)
        regions = to_windows(strip_labels, 1, plain_cols)
        hidden = from_windows(attend(blocks, regions, norm_gains[1], qkv_weight[0], proj_weight[0], rel_table[0]), 1, plain_cols)
        return feedforward(hidden, norm_gains[2], fc1_weight[0], fc2_weight[0])
    second_in = lax.map(plain_strip, (first_in.reshape(strip_rows, WIN, COLS, D), labels.reshape(strip_rows, WIN, COLS)))
    second_in = second_in.reshape(ROWS, COLS, D)
    margin = WIN - WIN // 2
    padded = jnp.pad(second_in, ((margin, margin), (margin, margin), (0, 0)))[:ROWS + WIN, :COLS + WIN]
    padded_labels = jnp.pad(labels, ((margin, margin), (margin, margin)))[:ROWS + WIN, :COLS + WIN]
    wide_cols = plain_cols + 1

    def shifted_strip(pieces):
        strip, strip_labels = pieces
        blocks = to_windows(strip, 1, wide_cols)
        regions = to_windows(strip_labels, 1, wide_cols)
        return from_windows(attend(blocks, regions, norm_gains[3], qkv_weight[1], proj_weight[1], rel_table[1]), 1, wide_cols)
    hidden = lax.map(shifted_strip, (padded.reshape(strip_rows + 1, WIN, COLS + WIN, D), padded_labels.reshape(strip_rows + 1, WIN, COLS + WIN)))
    hidden = hidden.reshape(ROWS + WIN, COLS + WIN, D)[margin:margin + ROWS, margin:margin + COLS]

    def finish_strip(strip):
        return feedforward(strip, norm_gains[4], fc1_weight[1], fc2_weight[1])
    return lax.map(finish_strip, hidden.reshape(strip_rows, WIN, COLS, D)).reshape(ROWS, COLS, D)
```

```python
import functools

import jax
import jax.numpy as jnp
from jax import lax
from jax.experimental import pallas as pl
from jax.experimental.pallas import tpu as pltpu
from jax.sharding import PartitionSpec as P

D = 128
HEADS = 4
HD = 32
WIN = 7
LAYERS = 5
C = 64

EPSILON = 1e-05

RIM = 12
F32 = jnp.float32
BF16 = jnp.bfloat16
NEG = -1e30
EXPS = HD ** (-0.5) * 1.4426950408889634


def norm(values, scales):
    centre = jnp.mean(values, -1, keepdims=True)
    centred = values - centre
    spread = jnp.mean(centred * centred, -1, keepdims=True)
    return centred * lax.rsqrt(spread + EPSILON) * scales


def dot(a, b):
    return jnp.dot(a, b, preferred_element_type=F32)


def silu(v):
    half = 0.5 * v
    return half + half * jnp.tanh(half)


def gelu(v):
    return 0.5 * v * (1.0 + lax.erf(v * 0.7071067811865476))


def kernel(
    trows,
    tcols,
    nrows,
    ncols,
    place_ref,
    planes_ref,
    wst_ref,
    wl_ref,
    e2_ref,
    gains_ref,
    qkv_ref,
    proj_ref,
    bias_ref,
    fc1_ref,
    fc2_ref,
    out_ref,
    raw,
    state,
    act_a,
    act_b,
    colmask,
    labels,
    t0,
    h1,
    h2,
):
    frows = trows + 2 * RIM
    fcols = tcols + 2 * RIM + 8
    pairs = frows // 2
    brows = trows + 2 * WIN
    wins0 = tcols // WIN + 2
    wins1 = tcols // WIN + 1

    row_at = place_ref[0] * trows - RIM
    col_at = place_ref[1] * tcols - RIM
    lane = lax.broadcasted_iota(jnp.int32, (1, 128), 1)
    low = lane < C

    raw[...] = jnp.zeros_like(raw)
    for c in range(4):
        raw[c, 8 : 8 + frows, :] = planes_ref[c].astype(F32)
    act_a[0] = jnp.zeros_like(act_a[0])
    act_b[0] = jnp.zeros_like(act_b[0])
    act_a[pairs + 1] = jnp.zeros_like(act_a[0])
    act_b[pairs + 1] = jnp.zeros_like(act_b[0])
    gcol = lax.broadcasted_iota(jnp.int32, (fcols, 128), 0) + col_at
    colmask[...] = ((gcol >= 0) & (gcol < ncols * tcols)).astype(F32)

    lab = planes_ref[4].astype(F32) + 1.0
    lab = jnp.concatenate([lab, jnp.zeros((2, fcols), F32)], 0).T
    for r in range(brows):
        labels[r, 0:fcols, :] = jnp.broadcast_to(lab[:, 5 + r : 6 + r], (fcols, 128))

    def rowmask(k):
        g = row_at + 2 * k
        ok0 = jnp.logical_and(g >= 0, g < nrows * trows).astype(F32)
        ok1 = jnp.logical_and(g >= -1, g < nrows * trows - 1).astype(F32)
        return jnp.where(low, ok0, ok1)

    def gathered(y):
        return (
            pltpu.roll(y[:, 0:128], 1, 0)
            + y[:, 128:256]
            + pltpu.roll(y[:, 256:384], fcols - 1, 0)
        )

    def act_of(x, k):
        return (silu(x) * (colmask[...] * rowmask(k))).astype(BF16)

    def stem(g, _):
        rows = [raw[c, pl.ds(pl.multiple_of(8 * g, 8), 24), :] for c in range(4)]
        for i in range(4):
            k = 4 * g + i
            lhs = jnp.concatenate([v[2 * i + 7 : 2 * i + 15] for v in rows], 0).astype(BF16)
            y = lax.dot_general(
                lhs, wst_ref[...], (((0,), (0,)), ((), ())), preferred_element_type=F32
            )
            x = gathered(y)
            state[k] = x
            act_a[k + 1] = act_of(x, k)
        return 0

    lax.fori_loop(0, (pairs + 3) // 4, stem, 0)

    spans = [(1, pairs, 6), (1, pairs, 6), (2, pairs - 2, 5), (2, pairs - 2, 5)]
    bufs = [act_a, act_b]
    for layer in range(LAYERS - 1):
        src, dst = bufs[layer % 2], bufs[(layer + 1) % 2]
        lo, hi, many = spans[layer]

        def conv(i, _, layer=layer, src=src, dst=dst, lo=lo, many=many):
            k0 = lo + many * i
            lhs = jnp.concatenate(
                [
                    jnp.concatenate(
                        [src[k0 + j + 1], jnp.where(low, src[k0 + j + 2], src[k0 + j])], 1
                    )
                    for j in range(many)
                ],
                0,
            )
            y = dot(lhs, wl_ref[layer])
            xs = []
            for j in range(many):
                k = k0 + j
                x = state[k] + gathered(y[fcols * j : fcols * j + fcols])
                if layer < LAYERS - 2:
                    state[k] = x
                    dst[k + 1] = act_of(x, k)
                else:
                    xs.append(x)
            if layer == LAYERS - 2:
                z = dot(jnp.concatenate(xs, 0).astype(BF16), e2_ref[...])
                g = gains_ref[0:1, :]
                for j in range(many):
                    r = 2 * (k0 + j) - 4
                    zz = z[fcols * j : fcols * j + fcols]
                    t0[r, 0:fcols, :] = norm(zz[:, 0:128], g).astype(BF16).astype(F32)
                    t0[r + 1, 0:fcols, :] = norm(zz[:, 128:256], g).astype(BF16).astype(F32)
            return 0

        lax.fori_loop(0, (hi - lo) // many, conv, 0)

    token = lax.broadcasted_iota(jnp.int32, (56, 128), 0)
    pad = (token & 7) == 7
    diag = (lax.broadcasted_iota(jnp.int32, (56, 128), 1) & 63) == token
    hm = [((lane >= 32 * h) & (lane < 32 * h + 32)) for h in range(HEADS)]
    hst = jnp.concatenate(
        [jnp.broadcast_to(m.astype(F32), (64, 128)) for m in hm], 0
    ).astype(BF16)
    even = (lane & 32) == 0
    zero8 = jnp.zeros((8, 128), F32)

    def attend(block, src, src_row, src_cols, lab_row, dst, dst_row, dst_cols):
        count = len(src_cols)
        x = jnp.concatenate(
            [src[pl.ds(src_row, 7), c : c + 8, :].reshape(56, 128) for c in src_cols], 0
        )
        y = norm(x, gains_ref[1 + 2 * block : 2 + 2 * block, :]).astype(BF16)
        qkv = dot(y, qkv_ref[block])
        scores, values = [], []
        for w in range(count):
            rows = slice(56 * w, 56 * w + 56)
            q = qkv[rows, 0:128]
            kk = jnp.concatenate([qkv[rows, 128:256], zero8], 0)
            vv = jnp.concatenate([qkv[rows, 256:384], zero8], 0)
            qs = jnp.concatenate([jnp.where(low, q, 0.0), jnp.where(low, 0.0, q)], 0).astype(BF16)
            ks = jnp.concatenate([jnp.where(even, kk, 0.0), jnp.where(even, 0.0, kk)], 0)
            vs = jnp.concatenate([jnp.where(even, vv, 0.0), jnp.where(even, 0.0, vv)], 0)
            values.append(vs.astype(BF16))
            scores.append(
                lax.dot_general(
                    qs, ks.astype(BF16), (((1,), (1,)), ((), ())), preferred_element_type=F32
                )
            )
        probs = []
        for w in range(count):
            c = src_cols[w]
            li = labels[pl.ds(lab_row, 7), c : c + 8, :].reshape(56, 128)
            li = jnp.where(pad, -1.0, li)
            lj = jnp.sum(jnp.where(diag, li, 0.0), 0, keepdims=True)
            same = li == lj
            ps = []
            for half in range(2):
                at = slice(128 * half, 128 * half + 128)
                sh = scores[w][56 * half : 56 * half + 56]
                sh = jnp.where(same, sh + bias_ref[block, :, at], NEG)
                m0 = jnp.max(jnp.where(low, sh, NEG), -1, keepdims=True)
                m1 = jnp.max(jnp.where(low, NEG, sh), -1, keepdims=True)
                ps.append(jnp.exp2((sh - jnp.where(low, m0, m1)) * EXPS))
            probs.append(ps)
        sums = dot(
            jnp.concatenate([jnp.concatenate(ps, 1) for ps in probs], 0).astype(BF16), hst
        )
        outs = []
        for w in range(count):
            o = dot(jnp.concatenate(probs[w], 0).astype(BF16), values[w])
            outs.append(jnp.where(low, o[0:56], o[56:112]))
        mixed = (jnp.concatenate(outs, 0) / sums).astype(BF16)
        res = x + dot(mixed, proj_ref[block])
        for w in range(count):
            c = dst_cols[w]
            dst[pl.ds(dst_row, 7), c : c + 8, :] = res[56 * w : 56 * w + 56].reshape(
                7, 8, 128
            )

    def feed(block, h):
        y = norm(h, gains_ref[2 + 2 * block : 3 + 2 * block, :]).astype(BF16)
        u = gelu(dot(y, fc1_ref[block])).astype(BF16)
        return h + dot(u, fc2_ref[block])

    def block0(a, _):
        for g in range(0, wins0, 6):
            cols = [5 + 7 * w for w in range(g, min(g + 6, wins0))]
            attend(0, t0, 7 * a + 1, cols, 7 * a, h1, 7 * a, cols)
        return 0

    lax.fori_loop(0, brows // WIN, block0, 0)

    span = tcols + 8

    def feed0(i, _):
        r = 3 + 7 * i
        h = h1[pl.ds(r, 7), 8 : 8 + span, :].reshape(7 * span, 128)
        t = feed(0, h).astype(BF16).astype(F32)
        h1[pl.ds(r, 7), 8 : 8 + span, :] = t.reshape(7, span, 128)
        return 0

    lax.fori_loop(0, (trows + WIN) // 7, feed0, 0)

    def block1(a, _):
        for g in range(0, wins1, 6):
            ws = range(g, min(g + 6, wins1))
            attend(
                1,
                h1,
                3 + 7 * a,
                [8 + 7 * w for w in ws],
                3 + 7 * a,
                h2,
                7 * a,
                [4 + 7 * w for w in ws],
            )
        return 0

    lax.fori_loop(0, trows // WIN + 1, block1, 0)

    def feed1(i, _):
        r = 7 * i
        h = h2[pl.ds(4 + r, 7), 8 : 8 + tcols, :].reshape(7 * tcols, 128)
        out_ref[pl.ds(r, 7)] = feed(1, h).astype(BF16).reshape(7, tcols, 128)
        return 0

    lax.fori_loop(0, trows // 7, feed1, 0)


def prepare(
    pattern_ref,
    _,
    stem_ref,
    layer0_ref,
    layer1_ref,
    layer2_ref,
    layer3_ref,
    embed_ref,
    table_ref,
    wst_ref,
    wl_ref,
    e2_ref,
    bias_ref,
    across,
):
    zero = jnp.zeros((C, C), F32)
    for layer, taps_ref in enumerate((layer0_ref, layer1_ref, layer2_ref, layer3_ref)):
        blocks = []
        for b in range(3):
            k0, k1, k2 = [taps_ref[0, 0, 3 * a + b].astype(F32) for a in range(3)]
            blocks.append(jnp.concatenate([k1, k2, zero, k0], 1))
            blocks.append(jnp.concatenate([k0, k1, k2, zero], 1))
        wl_ref[layer] = jnp.concatenate(blocks, 0).T.astype(BF16)

    pattern = pattern_ref[0]
    outer = jnp.logical_or(pattern == 0, pattern == 3)
    channel = lax.broadcasted_iota(jnp.int32, (4, 32), 0)
    lane = lax.broadcasted_iota(jnp.int32, (4, 32), 1)
    plane = jnp.where(
        channel == 0,
        pattern,
        jnp.where(
            channel == 1,
            jnp.where(outer, 1, 0),
            jnp.where(channel == 2, jnp.where(outer, 2, 3), 3 - pattern),
        ),
    )
    blocks = []
    for b in range(3):
        for p in range(2):
            total = jnp.zeros((C, 32), F32)
            for a in range(3):
                spread = (lane == 8 * plane + a + p).astype(BF16)
                total = total + dot(stem_ref[0, 3 * a + b], spread)
            blocks.append(total)
    wst_ref[...] = jnp.concatenate(blocks, 0).T.astype(BF16)

    embed = embed_ref[...]
    blank = jnp.zeros_like(embed)
    e2_ref[...] = jnp.concatenate(
        [jnp.concatenate([embed, blank], 1), jnp.concatenate([blank, embed], 1)], 0
    )

    table = table_ref[...] * HD**0.5
    part0 = table.astype(BF16)
    part1 = (table - part0.astype(F32)).astype(BF16)
    part2 = (table - part0.astype(F32) - part1.astype(F32)).astype(BF16)
    entry = lax.broadcasted_iota(jnp.int32, (table.shape[1], 128), 0)
    spot = lax.broadcasted_iota(jnp.int32, (table.shape[1], 128), 1)
    base = (12 - lax.shift_right_logical(spot, 3)) * 13 + 6 - (spot & 7)
    for c in range(8):
        pick = (entry == base + min(c, 6)).astype(BF16)
        across[c] = dot(part0, pick) + dot(part1, pick) + dot(part2, pick)
    low = lax.broadcasted_iota(jnp.int32, (1, 128), 1) < 64
    for block in range(2):
        for half in range(2):
            at = 4 * block + 2 * half
            g0 = across[:, at, :]
            g1 = across[:, at + 1, :]
            for r in range(7):
                back = (6 - r) * 8
                bias_ref[block, 8 * r : 8 * r + 8, 128 * half : 128 * half + 128] = jnp.where(
                    low, pltpu.roll(g0, (128 - back) % 128, 1), pltpu.roll(g1, (192 - back) % 128, 1)
                )


def prepared(pattern, candidate, stem_bank, layer_bank, embed_weight, rel_table):
    taps = [
        pl.BlockSpec((1, 1, 9, C, C), lambda i, p, c, n=n: (n, c[n + 1], 0, 0, 0))
        for n in range(LAYERS - 1)
    ]
    return pl.pallas_call(
        prepare,
        out_shape=[
            jax.ShapeDtypeStruct((32, 6 * C), BF16),
            jax.ShapeDtypeStruct((LAYERS - 1, 4 * C, 6 * C), BF16),
            jax.ShapeDtypeStruct((2 * C, 2 * D), BF16),
            jax.ShapeDtypeStruct((2, 56, HEADS * 64), F32),
        ],
        grid_spec=pltpu.PrefetchScalarGridSpec(
            num_scalar_prefetch=2,
            grid=(1,),
            in_specs=[pl.BlockSpec((1, 9, C, 4), lambda i, p, c: (c[0], 0, 0, 0))]
            + taps
            + [
                pl.BlockSpec((C, D), lambda i, p, c: (0, 0)),
                pl.BlockSpec((8, 169), lambda i, p, c: (0, 0)),
            ],
            out_specs=[
                pl.BlockSpec((32, 6 * C), lambda i, p, c: (0, 0)),
                pl.BlockSpec((LAYERS - 1, 4 * C, 6 * C), lambda i, p, c: (0, 0, 0)),
                pl.BlockSpec((2 * C, 2 * D), lambda i, p, c: (0, 0)),
                pl.BlockSpec((2, 56, HEADS * 64), lambda i, p, c: (0, 0, 0)),
            ],
            scratch_shapes=[pltpu.VMEM((8, 8, 128), F32)],
        ),
        compiler_params=pltpu.CompilerParams(vmem_limit_bytes=32 * 1024 * 1024),
        cost_estimate=pl.CostEstimate(
            flops=100_000_000, bytes_accessed=4_000_000, transcendentals=0
        ),
    )(
        pattern,
        candidate,
        stem_bank,
        layer_bank,
        layer_bank,
        layer_bank,
        layer_bank,
        embed_weight,
        rel_table.reshape(8, 169),
    )


def swaps(values, axis):
    size = lax.axis_size(axis)
    even = [(i, i ^ 1) for i in range(size)]
    odd = []
    for i in range(1, size - 1, 2):
        odd += [(i, i + 1), (i + 1, i)]
    first = lax.ppermute(values, axis, even)
    second = lax.ppermute(values, axis, odd)
    is_even = lax.axis_index(axis) % 2 == 0
    return jnp.where(is_even, second, first), jnp.where(is_even, first, second)


def computed(sizes, *arrays):
    trows, tcols = sizes[:2]
    frows, fcols = trows + 2 * RIM, tcols + 2 * RIM + 8
    pairs = frows // 2
    brows = trows + 2 * WIN
    vmem = pl.BlockSpec(memory_space=pltpu.VMEM)
    return pl.pallas_call(
        functools.partial(kernel, *sizes),
        out_shape=jax.ShapeDtypeStruct((trows, tcols, D), BF16),
        in_specs=[pl.BlockSpec(memory_space=pltpu.SMEM)] + [vmem] * 10,
        out_specs=vmem,
        scratch_shapes=[
            pltpu.VMEM((4, 8 + frows + 10, fcols), F32),
            pltpu.VMEM((pairs + 1, fcols, 128), F32),
            pltpu.VMEM((pairs + 2, fcols, 128), BF16),
            pltpu.VMEM((pairs + 2, fcols, 128), BF16),
            pltpu.VMEM((fcols, 128), F32),
            pltpu.VMEM((brows, fcols + 8, 128), F32),
            pltpu.VMEM((brows + 2, fcols + 8, 128), F32),
            pltpu.VMEM((brows, fcols + 8, 128), F32),
            pltpu.VMEM((trows + WIN, fcols, 128), F32),
        ],
        compiler_params=pltpu.CompilerParams(vmem_limit_bytes=56 * 1024 * 1024),
    )(*arrays)


def shards(
    planes,
    pattern,
    candidate,
    stem_bank,
    layer_bank,
    embed_weight,
    norm_gains,
    qkv_weight,
    proj_weight,
    rel_table,
    fc1_weight,
    fc2_weight,
    labels,
):
    trows, tcols = labels.shape
    nrows, ncols = lax.axis_size("row"), lax.axis_size("col")
    own = jnp.concatenate([planes, labels.astype(BF16)[None]], 0)
    above, below = swaps(own, "row")
    tall = jnp.concatenate([above[:, trows - RIM :], own, below[:, :RIM]], 1)
    ends = jnp.concatenate([tall[:, :, :RIM], tall[:, :, tcols - RIM :]], 2)
    left, right = swaps(ends, "col")
    blank = jnp.zeros((5, trows + 2 * RIM, 8), BF16)
    wide = jnp.concatenate([left[:, :, RIM:], tall, right[:, :, :RIM], blank], 2)

    wst, wl, e2, bias = prepared(
        pattern, candidate, stem_bank, layer_bank, embed_weight, rel_table
    )
    place = jnp.stack([lax.axis_index("row"), lax.axis_index("col")]).astype(jnp.int32)

    return computed(
        (trows, tcols, nrows, ncols),
        place,
        wide,
        wst,
        wl,
        e2,
        norm_gains,
        qkv_weight,
        proj_weight,
        bias,
        fc1_weight,
        fc2_weight,
    )


def solution(mesh):
    placed = (
        P(None, "row", "col"),
        P(),
        P(),
        P(),
        P(),
        P(),
        P(),
        P(),
        P(),
        P(),
        P(),
        P(),
        P("row", "col"),
    )
    return jax.shard_map(
        shards, mesh=mesh, in_specs=placed, out_specs=P("row", "col", None), check_vma=False
    )
```

```python
import functools

import jax
import jax.numpy as jnp
from jax import lax
from jax.experimental import pallas as pl
from jax.experimental.pallas import tpu as pltpu
from jax.sharding import PartitionSpec as P

D = 128
HEADS = 4
HD = 32
WIN = 7
LAYERS = 5
C = 64

EPSILON = 1e-05

RIM = 12
F32 = jnp.float32
BF16 = jnp.bfloat16
NEG = -1e30
LOG2E = 1.4426950408889634
ROOT_HALF = 0.7071067811865476
LIMIT = 1e25
VMEM = 60 * 1024 * 1024


def scaled(centred, scales):
    total = jnp.sum(centred * centred, -1, keepdims=True)
    return centred * lax.rsqrt(total + D * EPSILON) * (scales * D**0.5)


def norm(values, scales):
    return scaled(values - jnp.mean(values, -1, keepdims=True), scales)


def dot(a, b):
    return jnp.dot(a, b, preferred_element_type=F32)


def silu(v):
    half = 0.5 * v
    return half + half * jnp.tanh(half)


def kernel(
    trows,
    tcols,
    nrows,
    ncols,
    place_ref,
    tall_ref,
    left_ref,
    right_ref,
    wst_ref,
    e2_ref,
    gains_ref,
    wl_hbm,
    qkv_hbm,
    proj_hbm,
    bias_hbm,
    fc1_hbm,
    fc2_hbm,
    out_ref,
    wl_ref,
    qkv_ref,
    proj_ref,
    bias_ref,
    fc1_ref,
    fc2_ref,
    sems,
    raw,
    state,
    act_a,
    act_b,
    colmask,
    labels,
    t0,
    h1,
    h2,
    check,
):
    frows = trows + 2 * RIM
    fcols = tcols + 2 * RIM + 8
    pairs = frows // 2
    brows = trows + 2 * WIN
    wins0 = tcols // WIN + 2
    wins1 = tcols // WIN + 1

    row_at = place_ref[0] * trows - RIM
    col_at = place_ref[1] * tcols - RIM
    lane = lax.broadcasted_iota(jnp.int32, (1, 128), 1)
    low = lane < C

    sources = (wl_hbm, qkv_hbm, bias_hbm, proj_hbm, fc1_hbm, fc2_hbm)
    targets = (wl_ref, qkv_ref, bias_ref, proj_ref, fc1_ref, fc2_ref)
    copies = [
        pltpu.make_async_copy(source, target, sems.at[n])
        for n, (source, target) in enumerate(zip(sources, targets))
    ]
    for copy in copies:
        copy.start()

    raw[...] = jnp.zeros_like(raw)
    mine = jnp.concatenate(
        [
            left_ref[...].astype(F32)[:, :, RIM:],
            tall_ref[...].astype(F32),
            right_ref[...].astype(F32)[:, :, :RIM],
            jnp.zeros((frows, 5, 8), F32),
        ],
        2,
    )
    grow = lax.broadcasted_iota(jnp.int32, mine.shape, 0) + row_at
    gcol = lax.broadcasted_iota(jnp.int32, mine.shape, 2) + col_at
    inside = (grow >= 0) & (grow < nrows * trows) & (gcol >= 0) & (gcol < ncols * tcols)
    raw[1 : 1 + frows, 0:5, :] = jnp.where(inside, mine, 0.0)
    act_a[0] = jnp.zeros_like(act_a[0])
    act_b[0] = jnp.zeros_like(act_b[0])
    act_b[1] = jnp.zeros_like(act_b[0])
    act_a[pairs + 1] = jnp.zeros_like(act_a[0])
    act_b[pairs + 1] = jnp.zeros_like(act_b[0])
    gcol = lax.broadcasted_iota(jnp.int32, (fcols, 128), 0) + col_at
    colmask[...] = ((gcol >= 0) & (gcol < ncols * tcols)).astype(F32)

    def rowmask(k):
        g = row_at + 2 * k
        ok0 = jnp.logical_and(g >= 0, g < nrows * trows).astype(F32)
        ok1 = jnp.logical_and(g >= -1, g < nrows * trows - 1).astype(F32)
        return jnp.where(low, ok0, ok1)

    def gathered(y):
        return (
            pltpu.roll(y[:, 0:128], 1, 0)
            + y[:, 128:256]
            + pltpu.roll(y[:, 256:384], fcols - 1, 0)
        )

    def act_of(x, k):
        return (silu(x) * (colmask[...] * rowmask(k))).astype(BF16)

    def stem(g, _):
        for i in range(5):
            k = 5 * g + i
            lhs = raw[pl.ds(2 * k, 4)].reshape(32, fcols).astype(BF16)
            y = lax.dot_general(
                lhs, wst_ref[...], (((0,), (0,)), ((), ())), preferred_element_type=F32
            )
            x = gathered(y)
            state[k] = x
            act_a[k + 1] = act_of(x, k)
            labels[2 * k, 0:fcols, :] = y[:, 384:512]
            labels[2 * k + 1, 0:fcols, :] = y[:, 512:640]
        return 0

    lax.fori_loop(0, (pairs + 1) // 5, stem, 0)
    copies[0].wait()

    spans = [(1, pairs, 6), (1, pairs, 6), (2, pairs - 2, 5), (2, pairs - 2, 5)]
    bufs = [act_a, act_b]
    for layer in range(LAYERS - 1):
        src, dst = bufs[layer % 2], bufs[(layer + 1) % 2]
        lo, hi, many = spans[layer]

        def conv(i, _, layer=layer, src=src, dst=dst, lo=lo, many=many):
            k0 = lo + many * i
            lhs = jnp.concatenate(
                [
                    jnp.concatenate(
                        [src[k0 + j + 1], jnp.where(low, src[k0 + j + 2], src[k0 + j])], 1
                    )
                    for j in range(many)
                ],
                0,
            )
            y = dot(lhs, wl_ref[layer])
            xs = []
            for j in range(many):
                k = k0 + j
                x = state[k] + gathered(y[fcols * j : fcols * j + fcols])
                if layer < LAYERS - 2:
                    state[k] = x
                    dst[k + 1] = act_of(x, k)
                else:
                    xs.append(x)
            if layer == LAYERS - 2:
                x5 = jnp.concatenate(xs, 0).astype(BF16)
                z = dot(jnp.concatenate([x5, x5], 1), e2_ref[...])
                g = gains_ref[0:1, :]
                for j in range(many):
                    r = 2 * (k0 + j) - 4
                    zz = z[fcols * j : fcols * j + fcols]
                    t0[r, 0:fcols, :] = scaled(zz[:, 0:128], g)
                    t0[r + 1, 0:fcols, :] = scaled(zz[:, 128:256], g)
            return 0

        lax.fori_loop(0, (hi - lo) // many, conv, 0)

    token = lax.broadcasted_iota(jnp.int32, (56, 128), 0)
    pad = (token & 7) == 7
    diag = (lax.broadcasted_iota(jnp.int32, (56, 128), 1) & 63) == token
    hm = [((lane >= 32 * h) & (lane < 32 * h + 32)) for h in range(HEADS)]
    hst = jnp.concatenate(
        [jnp.broadcast_to(m.astype(F32), (64, 128)) for m in hm], 0
    ).astype(BF16)
    even = (lane & 32) == 0
    zero8 = jnp.zeros((8, 128), F32)

    def attend(block, exact, src, src_row, src_cols, lab_row, dst, dst_row, dst_cols):
        count = len(src_cols)
        x = jnp.concatenate(
            [src[pl.ds(src_row, 7), c : c + 8, :].reshape(56, 128) for c in src_cols], 0
        )
        y = norm(x, gains_ref[1 + 2 * block : 2 + 2 * block, :]).astype(BF16)
        qkv = dot(y, qkv_ref[block])
        scores, values = [], []
        for w in range(count):
            rows = slice(56 * w, 56 * w + 56)
            q = qkv[rows, 0:128] * (LOG2E * HD**-0.5)
            kk = jnp.concatenate([qkv[rows, 128:256], zero8], 0)
            vv = jnp.concatenate([qkv[rows, 256:384], zero8], 0)
            qs = jnp.concatenate([jnp.where(low, q, 0.0), jnp.where(low, 0.0, q)], 0).astype(BF16)
            ks = jnp.concatenate([jnp.where(even, kk, 0.0), jnp.where(even, 0.0, kk)], 0)
            vs = jnp.concatenate([jnp.where(even, vv, 0.0), jnp.where(even, 0.0, vv)], 0)
            values.append(vs.astype(BF16))
            scores.append(
                lax.dot_general(
                    qs, ks.astype(BF16), (((1,), (1,)), ((), ())), preferred_element_type=F32
                )
            )
        probs = []
        for w in range(count):
            c = src_cols[w]
            li = labels[pl.ds(lab_row, 7), c : c + 8, :].reshape(56, 128)
            li = jnp.where(pad, -1.0, li)
            lj = jnp.sum(jnp.where(diag, li, 0.0), 0, keepdims=True)
            same = li == lj
            ps = []
            for half in range(2):
                at = slice(128 * half, 128 * half + 128)
                sh = scores[w][56 * half : 56 * half + 56]
                sh = jnp.where(same, sh + bias_ref[block, :, at], NEG)
                if exact:
                    m0 = jnp.max(jnp.where(low, sh, NEG), -1, keepdims=True)
                    m1 = jnp.max(jnp.where(low, NEG, sh), -1, keepdims=True)
                    sh = sh - jnp.where(low, m0, m1)
                ps.append(jnp.exp2(sh))
            probs.append(ps)
        sums = dot(
            jnp.concatenate([jnp.concatenate(ps, 1) for ps in probs], 0).astype(BF16), hst
        )
        outs = []
        for w in range(count):
            o = dot(jnp.concatenate(probs[w], 0).astype(BF16), values[w])
            outs.append(jnp.where(low, o[0:56], o[56:112]))
        over = 1.0 / sums
        if not exact:
            worst = jnp.max(jnp.maximum(sums, over).reshape(7 * count, 8, 128), 0)
            check[...] = jnp.maximum(check[...], worst)
        mixed = (jnp.concatenate(outs, 0) * over).astype(BF16)
        res = x + dot(mixed, proj_ref[block])
        for w in range(count):
            c = dst_cols[w]
            dst[pl.ds(dst_row, 7), c : c + 8, :] = res[56 * w : 56 * w + 56].reshape(
                7, 8, 128
            )

    def feed(block, h):
        y = norm(h, gains_ref[2 + 2 * block : 3 + 2 * block, :] * ROOT_HALF).astype(BF16)
        v = dot(y, fc1_ref[block])
        u = (v * (1.0 + lax.erf(v))).astype(BF16)
        return h + dot(u, fc2_ref[block]) * ROOT_HALF

    def blocks(count, groups, block):
        check[...] = jnp.zeros_like(check)
        lax.fori_loop(0, count, lambda a, _: groups(a, False, block), 0)

        @pl.when(jnp.logical_not(jnp.max(check[...]) < LIMIT))
        def _():
            lax.fori_loop(0, count, lambda a, _: groups(a, True, block), 0)

    def groups0(a, exact, block):
        for g in range(0, wins0, 6):
            cols = [5 + 7 * w for w in range(g, min(g + 6, wins0))]
            attend(block, exact, t0, 7 * a + 1, cols, 7 * a + 5, h1, 7 * a, cols)
        return 0

    for copy in copies[1:4]:
        copy.wait()
    blocks(brows // WIN, groups0, 0)
    for copy in copies[4:6]:
        copy.wait()

    span = tcols + 8

    def feed0(i, _):
        r = 3 + 7 * i
        h = h1[pl.ds(r, 7), 8 : 8 + span, :].reshape(7 * span, 128)
        t = feed(0, h)
        h1[pl.ds(r, 7), 8 : 8 + span, :] = t.reshape(7, span, 128)
        return 0

    lax.fori_loop(0, (trows + WIN) // 7, feed0, 0)

    def groups1(a, exact, block):
        for g in range(0, wins1, 6):
            ws = range(g, min(g + 6, wins1))
            from_cols = [8 + 7 * w for w in ws]
            to_cols = [4 + 7 * w for w in ws]
            attend(block, exact, h1, 3 + 7 * a, from_cols, 8 + 7 * a, h2, 7 * a, to_cols)
        return 0

    blocks(trows // WIN + 1, groups1, 1)

    def feed1(i, _):
        r = 7 * i
        h = h2[pl.ds(4 + r, 7), 8 : 8 + tcols, :].reshape(7 * tcols, 128)
        out_ref[pl.ds(r, 7)] = feed(1, h).astype(BF16).reshape(7, tcols, 128)
        return 0

    lax.fori_loop(0, trows // 7, feed1, 0)


def prepare(
    pattern_ref,
    _,
    stem_ref,
    layer0_ref,
    layer1_ref,
    layer2_ref,
    layer3_ref,
    embed_ref,
    table_ref,
    wst_ref,
    wl_ref,
    e2_ref,
    bias_ref,
    across,
):
    zero = jnp.zeros((C, C), F32)
    for layer, taps_ref in enumerate((layer0_ref, layer1_ref, layer2_ref, layer3_ref)):
        blocks = []
        for b in range(3):
            k0, k1, k2 = [taps_ref[0, 0, 3 * a + b].astype(F32) for a in range(3)]
            blocks.append(jnp.concatenate([k1, k2, zero, k0], 1))
            blocks.append(jnp.concatenate([k0, k1, k2, zero], 1))
        wl_ref[layer] = jnp.concatenate(blocks, 0).T.astype(BF16)

    pattern = pattern_ref[0]
    outer = jnp.logical_or(pattern == 0, pattern == 3)
    row = lax.broadcasted_iota(jnp.int32, (32, 16), 0)
    channel = lax.broadcasted_iota(jnp.int32, (32, 16), 1)
    plane = jnp.where(
        channel == 0,
        pattern,
        jnp.where(
            channel == 1,
            jnp.where(outer, 1, 0),
            jnp.where(channel == 2, jnp.where(outer, 2, 3), 3 - pattern),
        ),
    )
    taps = [
        jnp.concatenate([stem_ref[0, t].astype(F32), jnp.zeros((12, C), F32)], 0).astype(BF16)
        for t in range(9)
    ]
    blocks = []
    for b in range(3):
        for p in range(2):
            total = jnp.zeros((32, C), F32)
            for a in range(3):
                spread = ((row == 8 * (a + p) + plane) & (channel < 4)).astype(BF16)
                total = total + dot(spread, taps[3 * a + b])
            blocks.append(total)
    row = lax.broadcasted_iota(jnp.int32, (32, 128), 0)
    for p in range(2):
        blocks.append((row == 8 * (1 + p) + 4).astype(F32))
    wst_ref[...] = jnp.concatenate(blocks, 1).astype(BF16)

    embed = embed_ref[...].astype(F32)
    embed = embed - jnp.mean(embed, -1, keepdims=True)
    high = embed.astype(BF16).astype(F32)
    blank = jnp.zeros_like(embed)
    e2_ref[...] = jnp.concatenate(
        [
            jnp.concatenate(pair, 1)
            for part in (high, embed - high)
            for pair in ((part, blank), (blank, part))
        ],
        0,
    ).astype(BF16)

    table = jnp.concatenate([table_ref[0], table_ref[1]], 0) * LOG2E
    table = jnp.concatenate([table, jnp.zeros((8, 256 - table.shape[1]), F32)], 1)
    part0 = table.astype(BF16)
    part1 = (table - part0.astype(F32)).astype(BF16)
    part2 = (table - part0.astype(F32) - part1.astype(F32)).astype(BF16)
    entry = lax.broadcasted_iota(jnp.int32, (table.shape[1], 128), 0)
    spot = lax.broadcasted_iota(jnp.int32, (table.shape[1], 128), 1)
    base = (12 - lax.shift_right_logical(spot, 3)) * 13 + 6 - (spot & 7)
    for c in range(8):
        pick = (entry == base + min(c, 6)).astype(BF16)
        across[c] = dot(part0, pick) + dot(part1, pick) + dot(part2, pick)
    low = lax.broadcasted_iota(jnp.int32, (1, 128), 1) < 64
    for block in range(2):
        for half in range(2):
            at = 4 * block + 2 * half
            g0 = across[:, at, :]
            g1 = across[:, at + 1, :]
            for r in range(7):
                back = (6 - r) * 8
                bias_ref[block, 8 * r : 8 * r + 8, 128 * half : 128 * half + 128] = jnp.where(
                    low, pltpu.roll(g0, (128 - back) % 128, 1), pltpu.roll(g1, (192 - back) % 128, 1)
                )


def prepared(pattern, candidate, stem_bank, layer_bank, embed_weight, rel_table):
    taps = [
        pl.BlockSpec((1, 1, 9, C, C), lambda i, p, c, n=n: (n, c[n + 1], 0, 0, 0))
        for n in range(LAYERS - 1)
    ]
    return pl.pallas_call(
        prepare,
        out_shape=[
            jax.ShapeDtypeStruct((32, 6 * C + 2 * D), BF16),
            jax.ShapeDtypeStruct((LAYERS - 1, 4 * C, 6 * C), BF16),
            jax.ShapeDtypeStruct((4 * C, 2 * D), BF16),
            jax.ShapeDtypeStruct((2, 56, HEADS * 64), F32),
        ],
        grid_spec=pltpu.PrefetchScalarGridSpec(
            num_scalar_prefetch=2,
            grid=(1,),
            in_specs=[pl.BlockSpec((1, 9, 4, C), lambda i, p, c: (c[0], 0, 0, 0))]
            + taps
            + [
                pl.BlockSpec((C, D), lambda i, p, c: (0, 0)),
                pl.BlockSpec((2, 4, 169), lambda i, p, c: (0, 0, 0)),
            ],
            out_specs=[
                pl.BlockSpec((32, 6 * C + 2 * D), lambda i, p, c: (0, 0)),
                pl.BlockSpec((LAYERS - 1, 4 * C, 6 * C), lambda i, p, c: (0, 0, 0)),
                pl.BlockSpec((4 * C, 2 * D), lambda i, p, c: (0, 0)),
                pl.BlockSpec((2, 56, HEADS * 64), lambda i, p, c: (0, 0, 0)),
            ],
            scratch_shapes=[pltpu.VMEM((8, 8, 128), F32)],
        ),
        compiler_params=pltpu.CompilerParams(vmem_limit_bytes=VMEM),
        cost_estimate=pl.CostEstimate(
            flops=100_000_000, bytes_accessed=4_000_000, transcendentals=0
        ),
    )(
        pattern,
        candidate,
        stem_bank.swapaxes(2, 3),
        layer_bank,
        layer_bank,
        layer_bank,
        layer_bank,
        embed_weight,
        rel_table,
    )


def swaps(values, axis):
    size = lax.axis_size(axis)
    even = [(i, i ^ 1) for i in range(size)]
    odd = [(i, ((i + 1) ^ 1) - 1) for i in range(size)]
    odd = [(i, j % size) for i, j in odd]
    return lax.ppermute(values, axis, even), lax.ppermute(values, axis, odd)


def ordered(pair, axis):
    first, second = pair
    is_even = lax.axis_index(axis) % 2 == 0
    return jnp.where(is_even, second, first), jnp.where(is_even, first, second)


def computed(sizes, *arrays):
    trows, tcols = sizes[:2]
    frows, fcols = trows + 2 * RIM, tcols + 2 * RIM + 8
    pairs = frows // 2
    brows = trows + 2 * WIN
    vmem = pl.BlockSpec(memory_space=pltpu.VMEM)
    return pl.pallas_call(
        functools.partial(kernel, *sizes),
        out_shape=jax.ShapeDtypeStruct((trows, tcols, D), BF16),
        in_specs=[pl.BlockSpec(memory_space=pltpu.SMEM)]
        + [vmem] * 6
        + [pl.BlockSpec(memory_space=pl.ANY)] * 6,
        out_specs=vmem,
        scratch_shapes=[
            pltpu.VMEM((LAYERS - 1, 4 * C, 6 * C), BF16),
            pltpu.VMEM((2, D, 3 * D), BF16),
            pltpu.VMEM((2, D, D), BF16),
            pltpu.VMEM((2, 56, HEADS * 64), F32),
            pltpu.VMEM((2, D, 4 * D), BF16),
            pltpu.VMEM((2, 4 * D, D), BF16),
            pltpu.SemaphoreType.DMA((6,)),
            pltpu.VMEM((frows + 6, 8, fcols), F32),
            pltpu.VMEM((pairs + 1, fcols, 128), F32),
            pltpu.VMEM((pairs + 2, fcols, 128), BF16),
            pltpu.VMEM((pairs + 2, fcols, 128), BF16),
            pltpu.VMEM((fcols, 128), F32),
            pltpu.VMEM((frows + 2, fcols + 8, 128), F32),
            pltpu.VMEM((brows + 2, fcols + 8, 128), F32),
            pltpu.VMEM((brows, fcols + 8, 128), F32),
            pltpu.VMEM((trows + WIN, fcols, 128), F32),
            pltpu.VMEM((8, 128), F32),
        ],
        compiler_params=pltpu.CompilerParams(vmem_limit_bytes=VMEM),
    )(*arrays)


def shards(
    planes,
    pattern,
    candidate,
    stem_bank,
    layer_bank,
    embed_weight,
    norm_gains,
    qkv_weight,
    proj_weight,
    rel_table,
    fc1_weight,
    fc2_weight,
    labels,
):
    trows, tcols = labels.shape
    nrows, ncols = lax.axis_size("row"), lax.axis_size("col")
    own = jnp.concatenate([planes.swapaxes(0, 1), labels.astype(BF16)[:, None]], 1)
    pair = swaps(own, "row")
    ready = prepared(pattern, candidate, stem_bank, layer_bank, embed_weight, rel_table)
    pair, (wst, wl, e2, bias) = lax.optimization_barrier((pair, ready))
    above, below = ordered(pair, "row")
    tall = jnp.concatenate([above[trows - RIM :], own, below[:RIM]], 0)
    ends = jnp.concatenate([tall[:, :, :RIM], tall[:, :, tcols - RIM :]], 2)
    left, right = ordered(swaps(ends, "col"), "col")
    place = jnp.stack([lax.axis_index("row"), lax.axis_index("col")]).astype(jnp.int32)

    return computed(
        (trows, tcols, nrows, ncols),
        place,
        tall,
        left,
        right,
        wst,
        e2,
        norm_gains,
        wl,
        qkv_weight,
        proj_weight,
        bias,
        fc1_weight,
        fc2_weight,
    )


def solution(mesh):
    placed = (
        P(None, "row", "col"),
        P(),
        P(),
        P(),
        P(),
        P(),
        P(),
        P(),
        P(),
        P(),
        P(),
        P(),
        P("row", "col"),
    )
    return jax.shard_map(
        shards, mesh=mesh, in_specs=placed, out_specs=P("row", "col", None), check_vma=False
    )
```

```python
import functools

import jax
import jax.numpy as jnp
from jax import lax
from jax.experimental import pallas as pl
from jax.experimental.pallas import tpu as pltpu
from jax.sharding import PartitionSpec as P

D = 128
HEADS = 4
HD = 32
WIN = 7
LAYERS = 5
C = 64

EPSILON = 1e-05

RIM = 12
F32 = jnp.float32
BF16 = jnp.bfloat16
NEG = -1e30
LOG2E = 1.4426950408889634
ROOT_HALF = 0.7071067811865476
LIMIT = 1e25
VMEM = 60 * 1024 * 1024


def scaled(centred, scales):
    total = jnp.sum(centred * centred, -1, keepdims=True)
    return centred * lax.rsqrt(total + D * EPSILON) * (scales * D**0.5)


def norm(values, scales):
    return scaled(values - jnp.mean(values, -1, keepdims=True), scales)


def dot(a, b):
    return jnp.dot(a, b, preferred_element_type=F32)


def silu(v):
    half = 0.5 * v
    return half + half * jnp.tanh(half)


def kernel(
    trows,
    tcols,
    nrows,
    ncols,
    place_ref,
    tall_ref,
    first_ref,
    second_ref,
    wst_ref,
    e2_ref,
    gains_ref,
    wl_hbm,
    qkv_hbm,
    proj_hbm,
    bias_hbm,
    fc1_hbm,
    fc2_hbm,
    out_ref,
    wl_ref,
    qkv_ref,
    proj_ref,
    bias_ref,
    fc1_ref,
    fc2_ref,
    sems,
    raw,
    state,
    act_a,
    act_b,
    colmask,
    labels,
    t0,
    h1,
    h2,
    check,
):
    frows = trows + 2 * RIM
    fcols = tcols + 2 * RIM + 8
    pairs = frows // 2
    brows = trows + 2 * WIN
    wins0 = tcols // WIN + 2
    wins1 = tcols // WIN + 1

    row_at = place_ref[0] * trows - RIM
    col_at = place_ref[1] * tcols - RIM
    lane = lax.broadcasted_iota(jnp.int32, (1, 128), 1)
    low = lane < C

    sources = (wl_hbm, qkv_hbm, bias_hbm, proj_hbm, fc1_hbm, fc2_hbm)
    targets = (wl_ref, qkv_ref, bias_ref, proj_ref, fc1_ref, fc2_ref)
    copies = [
        pltpu.make_async_copy(source, target, sems.at[n])
        for n, (source, target) in enumerate(zip(sources, targets))
    ]
    for copy in copies:
        copy.start()

    raw[...] = jnp.zeros_like(raw)
    even_col = lax.rem(place_ref[1], 2) == 0
    first = first_ref[...].astype(F32)
    second = second_ref[...].astype(F32)
    mine = jnp.concatenate(
        [
            jnp.where(even_col, second, first)[:, :, RIM:],
            tall_ref[...].astype(F32),
            jnp.where(even_col, first, second)[:, :, :RIM],
            jnp.zeros((frows, 5, 8), F32),
        ],
        2,
    )
    grow = lax.broadcasted_iota(jnp.int32, mine.shape, 0) + row_at
    gcol = lax.broadcasted_iota(jnp.int32, mine.shape, 2) + col_at
    inside = (grow >= 0) & (grow < nrows * trows) & (gcol >= 0) & (gcol < ncols * tcols)
    raw[1 : 1 + frows, 0:5, :] = jnp.where(inside, mine, 0.0)
    act_a[0] = jnp.zeros_like(act_a[0])
    act_b[0] = jnp.zeros_like(act_b[0])
    act_b[1] = jnp.zeros_like(act_b[0])
    act_a[pairs + 1] = jnp.zeros_like(act_a[0])
    act_b[pairs + 1] = jnp.zeros_like(act_b[0])
    gcol = lax.broadcasted_iota(jnp.int32, (fcols, 128), 0) + col_at
    colmask[...] = ((gcol >= 0) & (gcol < ncols * tcols)).astype(F32)

    def rowmask(k):
        g = row_at + 2 * k
        ok0 = jnp.logical_and(g >= 0, g < nrows * trows).astype(F32)
        ok1 = jnp.logical_and(g >= -1, g < nrows * trows - 1).astype(F32)
        return jnp.where(low, ok0, ok1)

    def gathered(y):
        return (
            pltpu.roll(y[:, 0:128], 1, 0)
            + y[:, 128:256]
            + pltpu.roll(y[:, 256:384], fcols - 1, 0)
        )

    def act_of(x, k):
        return (silu(x) * (colmask[...] * rowmask(k))).astype(BF16)

    def stem(g, _):
        for i in range(5):
            k = 5 * g + i
            lhs = raw[pl.ds(2 * k, 4)].reshape(32, fcols).astype(BF16)
            y = lax.dot_general(
                lhs, wst_ref[...], (((0,), (0,)), ((), ())), preferred_element_type=F32
            )
            x = gathered(y)
            state[k] = x
            act_a[k + 1] = act_of(x, k)
            both = y[:, 384:512]
            swapped = pltpu.roll(both, 64, 1)
            labels[2 * k, 0:fcols, :] = jnp.where(low, both, swapped)
            labels[2 * k + 1, 0:fcols, :] = jnp.where(low, swapped, both)
        return 0

    lax.fori_loop(0, (pairs + 1) // 5, stem, 0)
    copies[0].wait()

    spans = [(1, pairs, 9), (1, pairs, 9), (2, pairs - 2, 15), (2, pairs - 2, 15)]
    bufs = [act_a, act_b]
    for layer in range(LAYERS - 1):
        src, dst = bufs[layer % 2], bufs[(layer + 1) % 2]
        lo, hi, many = spans[layer]

        def conv(i, _, layer=layer, src=src, dst=dst, lo=lo, many=many):
            k0 = lo + many * i
            lhs = jnp.concatenate(
                [
                    jnp.concatenate(
                        [src[k0 + j + 1], jnp.where(low, src[k0 + j + 2], src[k0 + j])], 1
                    )
                    for j in range(many)
                ],
                0,
            )
            y = dot(lhs, wl_ref[layer])
            xs = []
            for j in range(many):
                k = k0 + j
                x = state[k] + gathered(y[fcols * j : fcols * j + fcols])
                if layer < LAYERS - 2:
                    state[k] = x
                    dst[k + 1] = act_of(x, k)
                else:
                    xs.append(x)
            if layer == LAYERS - 2:
                x5 = jnp.concatenate(xs, 0).astype(BF16)
                z = dot(jnp.concatenate([x5, x5], 1), e2_ref[...])
                g = gains_ref[0:1, :]
                for j in range(many):
                    r = 2 * (k0 + j) - 4
                    zz = z[fcols * j : fcols * j + fcols]
                    t0[r, 0:fcols, :] = scaled(zz[:, 0:128], g)
                    t0[r + 1, 0:fcols, :] = scaled(zz[:, 128:256], g)
            return 0

        lax.fori_loop(0, (hi - lo) // many, conv, 0)

    token = lax.broadcasted_iota(jnp.int32, (56, 128), 0)
    pad = (token & 7) == 7
    diag = (lax.broadcasted_iota(jnp.int32, (56, 128), 1) & 63) == token
    even = (lane & 32) == 0
    zero8 = jnp.zeros((8, 128), F32)

    def attend(block, exact, src, src_row, src_cols, lab_row, dst, dst_row, dst_cols):
        count = len(src_cols)
        x = jnp.concatenate(
            [src[pl.ds(src_row, 7), c : c + 8, :].reshape(56, 128) for c in src_cols], 0
        )
        y = norm(x, gains_ref[1 + 2 * block : 2 + 2 * block, :]).astype(BF16)
        qkv = dot(y, qkv_ref[block])
        scores, values = [], []
        for w in range(count):
            rows = slice(56 * w, 56 * w + 56)
            q = qkv[rows, 0:128] * (LOG2E * HD**-0.5)
            kk = jnp.concatenate([qkv[rows, 128:256], zero8], 0)
            vv = jnp.concatenate([qkv[rows, 256:384], zero8], 0)
            qs = jnp.concatenate([jnp.where(low, q, 0.0), jnp.where(low, 0.0, q)], 0).astype(BF16)
            ks = jnp.concatenate([jnp.where(even, kk, 0.0), jnp.where(even, 0.0, kk)], 0)
            vs = jnp.concatenate([jnp.where(even, vv, 0.0), jnp.where(even, 0.0, vv)], 0)
            values.append(vs.astype(BF16))
            scores.append(
                lax.dot_general(
                    qs, ks.astype(BF16), (((1,), (1,)), ((), ())), preferred_element_type=F32
                )
            )
        probs = []
        most = jnp.ones((8, 128), F32)
        least = jnp.ones((8, 128), F32)
        for w in range(count):
            c = src_cols[w]
            li = labels[pl.ds(lab_row, 7), c : c + 8, :].reshape(56, 128)
            li = jnp.where(pad, -1.0, li)
            lj = jnp.sum(jnp.where(diag, li, 0.0), 0, keepdims=True)
            same = li == lj
            ps = []
            for half in range(2):
                at = slice(128 * half, 128 * half + 128)
                sh = scores[w][56 * half : 56 * half + 56]
                sh = jnp.where(same, sh + bias_ref[block, :, at], NEG)
                if exact:
                    m0 = jnp.max(jnp.where(low, sh, NEG), -1, keepdims=True)
                    m1 = jnp.max(jnp.where(low, NEG, sh), -1, keepdims=True)
                    sh = sh - jnp.where(low, m0, m1)
                ps.append(jnp.exp2(sh))
            for half in range(2):
                l0 = jnp.sum(jnp.where(low, ps[half], 0.0), -1, keepdims=True)
                l1 = jnp.sum(jnp.where(low, 0.0, ps[half]), -1, keepdims=True)
                over = 1.0 / jnp.where(low, l0, l1)
                if not exact:
                    folded = over.reshape(7, 8, 128)
                    most = jnp.maximum(most, jnp.max(folded, 0))
                    least = jnp.minimum(least, jnp.min(folded, 0))
                ps[half] = ps[half] * over
            probs.append(ps)
        outs = []
        for w in range(count):
            o = dot(jnp.concatenate(probs[w], 0).astype(BF16), values[w])
            outs.append(jnp.where(low, o[0:56], o[56:112]))
        if not exact:
            check[...] = jnp.maximum(check[...], jnp.maximum(most, 1.0 / least))
        mixed = jnp.concatenate(outs, 0).astype(BF16)
        res = x + dot(mixed, proj_ref[block])
        for w in range(count):
            c = dst_cols[w]
            dst[pl.ds(dst_row, 7), c : c + 8, :] = res[56 * w : 56 * w + 56].reshape(
                7, 8, 128
            )

    def feed(block, h):
        y = norm(h, gains_ref[2 + 2 * block : 3 + 2 * block, :] * ROOT_HALF).astype(BF16)
        v = dot(y, fc1_ref[block])
        u = (v * (1.0 + lax.erf(v))).astype(BF16)
        return h + dot(u, fc2_ref[block]) * ROOT_HALF

    def blocks(count, groups, block):
        check[...] = jnp.zeros_like(check)
        lax.fori_loop(0, count, lambda a, _: groups(a, False, block), 0)

        @pl.when(jnp.logical_not(jnp.max(check[...]) < LIMIT))
        def _():
            lax.fori_loop(0, count, lambda a, _: groups(a, True, block), 0)

    def groups0(a, exact, block):
        for g in range(0, wins0, 18):
            cols = [5 + 7 * w for w in range(g, min(g + 18, wins0))]
            attend(block, exact, t0, 7 * a + 1, cols, 7 * a + 5, h1, 7 * a, cols)
        return 0

    for copy in copies[1:4]:
        copy.wait()
    blocks(brows // WIN, groups0, 0)
    for copy in copies[4:6]:
        copy.wait()

    span = tcols + 8

    def feed0(i, _):
        r = 3 + 21 * i
        h = h1[pl.ds(r, 21), 8 : 8 + span, :].reshape(21 * span, 128)
        t = feed(0, h)
        h1[pl.ds(r, 21), 8 : 8 + span, :] = t.reshape(21, span, 128)
        return 0

    lax.fori_loop(0, (trows + WIN) // 21, feed0, 0)

    def groups1(a, exact, block):
        for g in range(0, wins1, 18):
            ws = range(g, min(g + 18, wins1))
            from_cols = [8 + 7 * w for w in ws]
            to_cols = [4 + 7 * w for w in ws]
            attend(block, exact, h1, 3 + 7 * a, from_cols, 8 + 7 * a, h2, 7 * a, to_cols)
        return 0

    blocks(trows // WIN + 1, groups1, 1)

    def feed1(i, _):
        r = 14 * i
        h = h2[pl.ds(4 + r, 14), 8 : 8 + tcols, :].reshape(14 * tcols, 128)
        out_ref[pl.ds(r, 14)] = feed(1, h).astype(BF16).reshape(14, tcols, 128)
        return 0

    lax.fori_loop(0, trows // 14, feed1, 0)


def prepare(
    pattern_ref,
    _,
    stem_ref,
    layer0_ref,
    layer1_ref,
    layer2_ref,
    layer3_ref,
    embed_ref,
    table_ref,
    wst_ref,
    wl_ref,
    e2_ref,
    bias_ref,
    across,
):
    zero = jnp.zeros((C, C), F32)
    for layer, taps_ref in enumerate((layer0_ref, layer1_ref, layer2_ref, layer3_ref)):
        blocks = []
        for b in range(3):
            k0, k1, k2 = [taps_ref[0, 0, 3 * a + b].astype(F32) for a in range(3)]
            blocks.append(jnp.concatenate([k1, k2, zero, k0], 1))
            blocks.append(jnp.concatenate([k0, k1, k2, zero], 1))
        wl_ref[layer] = jnp.concatenate(blocks, 0).T.astype(BF16)

    pattern = pattern_ref[0]
    outer = jnp.logical_or(pattern == 0, pattern == 3)
    row = lax.broadcasted_iota(jnp.int32, (32, 16), 0)
    channel = lax.broadcasted_iota(jnp.int32, (32, 16), 1)
    plane = jnp.where(
        channel == 0,
        pattern,
        jnp.where(
            channel == 1,
            jnp.where(outer, 1, 0),
            jnp.where(channel == 2, jnp.where(outer, 2, 3), 3 - pattern),
        ),
    )
    taps = [
        jnp.concatenate([stem_ref[0, t].astype(F32), jnp.zeros((12, C), F32)], 0).astype(BF16)
        for t in range(9)
    ]
    blocks = []
    for b in range(3):
        for p in range(2):
            total = jnp.zeros((32, C), F32)
            for a in range(3):
                spread = ((row == 8 * (a + p) + plane) & (channel < 4)).astype(BF16)
                total = total + dot(spread, taps[3 * a + b])
            blocks.append(total)
    row = lax.broadcasted_iota(jnp.int32, (32, C), 0)
    for p in range(2):
        blocks.append((row == 8 * (1 + p) + 4).astype(F32))
    wst_ref[...] = jnp.concatenate(blocks, 1).astype(BF16)

    embed = embed_ref[...].astype(F32)
    embed = embed - jnp.mean(embed, -1, keepdims=True)
    high = embed.astype(BF16).astype(F32)
    blank = jnp.zeros_like(embed)
    e2_ref[...] = jnp.concatenate(
        [
            jnp.concatenate(pair, 1)
            for part in (high, embed - high)
            for pair in ((part, blank), (blank, part))
        ],
        0,
    ).astype(BF16)

    table = jnp.concatenate([table_ref[0], table_ref[1]], 0) * LOG2E
    table = jnp.concatenate([table, jnp.zeros((8, 256 - table.shape[1]), F32)], 1)
    part0 = table.astype(BF16)
    part1 = (table - part0.astype(F32)).astype(BF16)
    part2 = (table - part0.astype(F32) - part1.astype(F32)).astype(BF16)
    entry = lax.broadcasted_iota(jnp.int32, (table.shape[1], 128), 0)
    spot = lax.broadcasted_iota(jnp.int32, (table.shape[1], 128), 1)
    base = (12 - lax.shift_right_logical(spot, 3)) * 13 + 6 - (spot & 7)
    for c in range(8):
        pick = (entry == base + min(c, 6)).astype(BF16)
        across[c] = dot(part0, pick) + dot(part1, pick) + dot(part2, pick)
    low = lax.broadcasted_iota(jnp.int32, (1, 128), 1) < 64
    for block in range(2):
        for half in range(2):
            at = 4 * block + 2 * half
            g0 = across[:, at, :]
            g1 = across[:, at + 1, :]
            for r in range(7):
                back = (6 - r) * 8
                bias_ref[block, 8 * r : 8 * r + 8, 128 * half : 128 * half + 128] = jnp.where(
                    low, pltpu.roll(g0, (128 - back) % 128, 1), pltpu.roll(g1, (192 - back) % 128, 1)
                )


def prepared(pattern, candidate, stem_bank, layer_bank, embed_weight, rel_table):
    taps = [
        pl.BlockSpec((1, 1, 9, C, C), lambda i, p, c, n=n: (n, c[n + 1], 0, 0, 0))
        for n in range(LAYERS - 1)
    ]
    return pl.pallas_call(
        prepare,
        out_shape=[
            jax.ShapeDtypeStruct((32, 8 * C), BF16),
            jax.ShapeDtypeStruct((LAYERS - 1, 4 * C, 6 * C), BF16),
            jax.ShapeDtypeStruct((4 * C, 2 * D), BF16),
            jax.ShapeDtypeStruct((2, 56, HEADS * 64), F32),
        ],
        grid_spec=pltpu.PrefetchScalarGridSpec(
            num_scalar_prefetch=2,
            grid=(1,),
            in_specs=[pl.BlockSpec((1, 9, 4, C), lambda i, p, c: (c[0], 0, 0, 0))]
            + taps
            + [
                pl.BlockSpec((C, D), lambda i, p, c: (0, 0)),
                pl.BlockSpec((2, 4, 169), lambda i, p, c: (0, 0, 0)),
            ],
            out_specs=[
                pl.BlockSpec((32, 8 * C), lambda i, p, c: (0, 0)),
                pl.BlockSpec((LAYERS - 1, 4 * C, 6 * C), lambda i, p, c: (0, 0, 0)),
                pl.BlockSpec((4 * C, 2 * D), lambda i, p, c: (0, 0)),
                pl.BlockSpec((2, 56, HEADS * 64), lambda i, p, c: (0, 0, 0)),
            ],
            scratch_shapes=[pltpu.VMEM((8, 8, 128), F32)],
        ),
        compiler_params=pltpu.CompilerParams(vmem_limit_bytes=VMEM),
        cost_estimate=pl.CostEstimate(
            flops=100_000_000, bytes_accessed=4_000_000, transcendentals=0
        ),
    )(
        pattern,
        candidate,
        stem_bank.swapaxes(2, 3),
        layer_bank,
        layer_bank,
        layer_bank,
        layer_bank,
        embed_weight,
        rel_table,
    )


def swaps(values, axis):
    size = lax.axis_size(axis)
    even = [(i, i ^ 1) for i in range(size)]
    odd = [(i, ((i + 1) ^ 1) - 1) for i in range(size)]
    odd = [(i, j % size) for i, j in odd]
    return lax.ppermute(values, axis, even), lax.ppermute(values, axis, odd)


def ordered(pair, axis):
    first, second = pair
    is_even = lax.axis_index(axis) % 2 == 0
    return jnp.where(is_even, second, first), jnp.where(is_even, first, second)


def computed(sizes, *arrays):
    trows, tcols = sizes[:2]
    frows, fcols = trows + 2 * RIM, tcols + 2 * RIM + 8
    pairs = frows // 2
    brows = trows + 2 * WIN
    vmem = pl.BlockSpec(memory_space=pltpu.VMEM)
    return pl.pallas_call(
        functools.partial(kernel, *sizes),
        out_shape=jax.ShapeDtypeStruct((trows, tcols, D), BF16),
        in_specs=[pl.BlockSpec(memory_space=pltpu.SMEM)]
        + [vmem] * 6
        + [pl.BlockSpec(memory_space=pl.ANY)] * 6,
        out_specs=vmem,
        scratch_shapes=[
            pltpu.VMEM((LAYERS - 1, 4 * C, 6 * C), BF16),
            pltpu.VMEM((2, D, 3 * D), BF16),
            pltpu.VMEM((2, D, D), BF16),
            pltpu.VMEM((2, 56, HEADS * 64), F32),
            pltpu.VMEM((2, D, 4 * D), BF16),
            pltpu.VMEM((2, 4 * D, D), BF16),
            pltpu.SemaphoreType.DMA((6,)),
            pltpu.VMEM((frows + 6, 8, fcols), F32),
            pltpu.VMEM((pairs + 1, fcols, 128), F32),
            pltpu.VMEM((pairs + 2, fcols, 128), BF16),
            pltpu.VMEM((pairs + 2, fcols, 128), BF16),
            pltpu.VMEM((fcols, 128), F32),
            pltpu.VMEM((frows + 2, fcols + 8, 128), F32),
            pltpu.VMEM((brows + 2, fcols + 8, 128), F32),
            pltpu.VMEM((brows, fcols + 8, 128), F32),
            pltpu.VMEM((trows + WIN, fcols, 128), F32),
            pltpu.VMEM((8, 128), F32),
        ],
        compiler_params=pltpu.CompilerParams(vmem_limit_bytes=VMEM),
    )(*arrays)


def shards(
    planes,
    pattern,
    candidate,
    stem_bank,
    layer_bank,
    embed_weight,
    norm_gains,
    qkv_weight,
    proj_weight,
    rel_table,
    fc1_weight,
    fc2_weight,
    labels,
):
    trows, tcols = labels.shape
    nrows, ncols = lax.axis_size("row"), lax.axis_size("col")
    own = jnp.concatenate([planes.swapaxes(0, 1), labels.astype(BF16)[:, None]], 1)
    pair = swaps(own, "row")
    ready = prepared(pattern, candidate, stem_bank, layer_bank, embed_weight, rel_table)
    pair, (wst, wl, e2, bias) = (pair, ready)
    above, below = ordered(pair, "row")
    tall = jnp.concatenate([above[trows - RIM :], own, below[:RIM]], 0)
    ends = jnp.concatenate([tall[:, :, :RIM], tall[:, :, tcols - RIM :]], 2)
    first, second = swaps(ends, "col")
    place = jnp.stack([lax.axis_index("row"), lax.axis_index("col")]).astype(jnp.int32)

    return computed(
        (trows, tcols, nrows, ncols),
        place,
        tall,
        first,
        second,
        wst,
        e2,
        norm_gains,
        wl,
        qkv_weight,
        proj_weight,
        bias,
        fc1_weight,
        fc2_weight,
    )


def solution(mesh):
    placed = (
        P(None, "row", "col"),
        P(),
        P(),
        P(),
        P(),
        P(),
        P(),
        P(),
        P(),
        P(),
        P(),
        P(),
        P("row", "col"),
    )
    return jax.shard_map(
        shards, mesh=mesh, in_specs=placed, out_specs=P("row", "col", None), check_vma=False
    )
```

```python
import functools

import jax
import jax.numpy as jnp
from jax import lax
from jax.experimental import pallas as pl
from jax.experimental.pallas import tpu as pltpu
from jax.sharding import PartitionSpec as P

D = 128
HEADS = 4
HD = 32
WIN = 7
LAYERS = 5
C = 64

EPSILON = 1e-05

RIM = 12
F32 = jnp.float32
BF16 = jnp.bfloat16
NEG = -1e30
LOG2E = 1.4426950408889634
ROOT_HALF = 0.7071067811865476
LIMIT = 1e25
VMEM = 60 * 1024 * 1024


def scaled(centred, scales):
    total = jnp.sum(centred * centred, -1, keepdims=True)
    return centred * lax.rsqrt(total + D * EPSILON) * (scales * D**0.5)


def norm(values, scales):
    return scaled(values - jnp.mean(values, -1, keepdims=True), scales)


def dot(a, b):
    return jnp.dot(a, b, preferred_element_type=F32)


def silu(v):
    half = 0.5 * v
    return half + half * jnp.tanh(half)


def kernel(
    trows,
    tcols,
    nrows,
    ncols,
    place_ref,
    tall_ref,
    first_ref,
    second_ref,
    wst_ref,
    e2_ref,
    gains_ref,
    wl_hbm,
    qkv_hbm,
    proj_hbm,
    bias_hbm,
    fc1_hbm,
    fc2_hbm,
    out_ref,
    wl_ref,
    qkv_ref,
    proj_ref,
    bias_ref,
    fc1_ref,
    fc2_ref,
    sems,
    raw,
    state,
    act_a,
    act_b,
    colmask,
    labels,
    t0,
    h1,
    h2,
    check,
):
    frows = trows + 2 * RIM
    fcols = tcols + 2 * RIM + 8
    pairs = frows // 2
    brows = trows + 2 * WIN
    wins0 = tcols // WIN + 2
    wins1 = tcols // WIN + 1

    row_at = place_ref[0] * trows - RIM
    col_at = place_ref[1] * tcols - RIM
    lane = lax.broadcasted_iota(jnp.int32, (1, 128), 1)
    low = lane < C

    sources = (wl_hbm, qkv_hbm, bias_hbm, proj_hbm, fc1_hbm, fc2_hbm)
    targets = (wl_ref, qkv_ref, bias_ref, proj_ref, fc1_ref, fc2_ref)
    copies = [
        pltpu.make_async_copy(source, target, sems.at[n])
        for n, (source, target) in enumerate(zip(sources, targets))
    ]
    for copy in copies:
        copy.start()

    raw[...] = jnp.zeros_like(raw)
    even_col = lax.rem(place_ref[1], 2) == 0
    first = first_ref[...].astype(F32)
    second = second_ref[...].astype(F32)
    mine = jnp.concatenate(
        [
            jnp.where(even_col, second, first)[:, :, RIM:],
            tall_ref[...].astype(F32),
            jnp.where(even_col, first, second)[:, :, :RIM],
            jnp.zeros((frows, 5, 8), F32),
        ],
        2,
    )
    grow = lax.broadcasted_iota(jnp.int32, mine.shape, 0) + row_at
    gcol = lax.broadcasted_iota(jnp.int32, mine.shape, 2) + col_at
    inside = (grow >= 0) & (grow < nrows * trows) & (gcol >= 0) & (gcol < ncols * tcols)
    raw[1 : 1 + frows, 0:5, :] = jnp.where(inside, mine, 0.0)
    act_a[0] = jnp.zeros_like(act_a[0])
    act_b[0] = jnp.zeros_like(act_b[0])
    act_b[1] = jnp.zeros_like(act_b[0])
    act_a[pairs + 1] = jnp.zeros_like(act_a[0])
    act_b[pairs + 1] = jnp.zeros_like(act_b[0])
    gcol = lax.broadcasted_iota(jnp.int32, (fcols, 128), 0) + col_at
    colmask[...] = ((gcol >= 0) & (gcol < ncols * tcols)).astype(F32)

    def rowmask(k):
        g = row_at + 2 * k
        ok0 = jnp.logical_and(g >= 0, g < nrows * trows).astype(F32)
        ok1 = jnp.logical_and(g >= -1, g < nrows * trows - 1).astype(F32)
        return jnp.where(low, ok0, ok1)

    def gathered(y):
        return (
            pltpu.roll(y[:, 0:128], 1, 0)
            + y[:, 128:256]
            + pltpu.roll(y[:, 256:384], fcols - 1, 0)
        )

    def act_of(x, k):
        return (silu(x) * (colmask[...] * rowmask(k))).astype(BF16)

    def stem(g, _):
        for i in range(5):
            k = 5 * g + i
            lhs = raw[pl.ds(2 * k, 4)].reshape(32, fcols).astype(BF16)
            y = lax.dot_general(
                lhs, wst_ref[...], (((0,), (0,)), ((), ())), preferred_element_type=F32
            )
            x = gathered(y)
            state[k] = x
            act_a[k + 1] = act_of(x, k)
            both = y[:, 384:512]
            swapped = pltpu.roll(both, 64, 1)
            labels[2 * k, 0:fcols, :] = jnp.where(low, both, swapped)
            labels[2 * k + 1, 0:fcols, :] = jnp.where(low, swapped, both)
        return 0

    lax.fori_loop(0, (pairs + 1) // 5, stem, 0)
    copies[0].wait()

    spans = [(1, pairs, 9), (1, pairs, 9), (2, pairs - 2, 15), (2, pairs - 2, 15)]
    bufs = [act_a, act_b]
    for layer in range(LAYERS - 1):
        src, dst = bufs[layer % 2], bufs[(layer + 1) % 2]
        lo, hi, many = spans[layer]

        def conv(i, _, layer=layer, src=src, dst=dst, lo=lo, many=many):
            k0 = lo + many * i
            lhs = jnp.concatenate(
                [
                    jnp.concatenate(
                        [src[k0 + j + 1], jnp.where(low, src[k0 + j + 2], src[k0 + j])], 1
                    )
                    for j in range(many)
                ],
                0,
            )
            y = dot(lhs, wl_ref[layer])
            xs = []
            for j in range(many):
                k = k0 + j
                x = state[k] + gathered(y[fcols * j : fcols * j + fcols])
                if layer < LAYERS - 2:
                    state[k] = x
                    dst[k + 1] = act_of(x, k)
                else:
                    xs.append(x)
            if layer == LAYERS - 2:
                x5 = jnp.concatenate(xs, 0).astype(BF16)
                z = dot(jnp.concatenate([x5, x5], 1), e2_ref[...])
                g = gains_ref[0:1, :]
                for j in range(many):
                    r = 2 * (k0 + j) - 4
                    zz = z[fcols * j : fcols * j + fcols]
                    t0[r, 0:fcols, :] = scaled(zz[:, 0:128], g)
                    t0[r + 1, 0:fcols, :] = scaled(zz[:, 128:256], g)
            return 0

        lax.fori_loop(0, (hi - lo) // many, conv, 0)

    token = lax.broadcasted_iota(jnp.int32, (56, 128), 0)
    pad = (token & 7) == 7
    diag = (lax.broadcasted_iota(jnp.int32, (56, 128), 1) & 63) == token
    even = (lane & 32) == 0
    zero8 = jnp.zeros((8, 128), F32)

    def attend(block, exact, src, src_row, src_cols, lab_row, dst, dst_row, dst_cols):
        count = len(src_cols)
        x = jnp.concatenate(
            [src[pl.ds(src_row, 7), c : c + 8, :].reshape(56, 128) for c in src_cols], 0
        )
        y = norm(x, gains_ref[1 + 2 * block : 2 + 2 * block, :]).astype(BF16)
        qkv = dot(y, qkv_ref[block])
        scores, values = [], []
        for w in range(count):
            rows = slice(56 * w, 56 * w + 56)
            q = qkv[rows, 0:128] * (LOG2E * HD**-0.5)
            kk = jnp.concatenate([qkv[rows, 128:256], zero8], 0)
            vv = jnp.concatenate([qkv[rows, 256:384], zero8], 0)
            qs = jnp.concatenate([jnp.where(low, q, 0.0), jnp.where(low, 0.0, q)], 0).astype(BF16)
            ks = jnp.concatenate([jnp.where(even, kk, 0.0), jnp.where(even, 0.0, kk)], 0)
            vs = jnp.concatenate([jnp.where(even, vv, 0.0), jnp.where(even, 0.0, vv)], 0)
            values.append(vs.astype(BF16))
            scores.append(
                lax.dot_general(
                    qs, ks.astype(BF16), (((1,), (1,)), ((), ())), preferred_element_type=F32
                )
            )
        probs = []
        most = jnp.ones((8, 128), F32)
        least = jnp.ones((8, 128), F32)
        for w in range(count):
            c = src_cols[w]
            li = labels[pl.ds(lab_row, 7), c : c + 8, :].reshape(56, 128)
            li = jnp.where(pad, -1.0, li)
            lj = jnp.sum(jnp.where(diag, li, 0.0), 0, keepdims=True)
            same = li == lj
            ps = []
            for half in range(2):
                at = slice(128 * half, 128 * half + 128)
                sh = scores[w][56 * half : 56 * half + 56]
                sh = jnp.where(same, sh + bias_ref[block, :, at], NEG)
                if exact:
                    m0 = jnp.max(jnp.where(low, sh, NEG), -1, keepdims=True)
                    m1 = jnp.max(jnp.where(low, NEG, sh), -1, keepdims=True)
                    sh = sh - jnp.where(low, m0, m1)
                ps.append(jnp.exp2(sh))
            for half in range(2):
                l0 = jnp.sum(jnp.where(low, ps[half], 0.0), -1, keepdims=True)
                l1 = jnp.sum(jnp.where(low, 0.0, ps[half]), -1, keepdims=True)
                over = 1.0 / jnp.where(low, l0, l1)
                if not exact:
                    folded = over.reshape(7, 8, 128)
                    most = jnp.maximum(most, jnp.max(folded, 0))
                    least = jnp.minimum(least, jnp.min(folded, 0))
                ps[half] = ps[half] * over
            probs.append(ps)
        outs = []
        for w in range(count):
            o = dot(jnp.concatenate(probs[w], 0).astype(BF16), values[w])
            outs.append(jnp.where(low, o[0:56], o[56:112]))
        if not exact:
            check[...] = jnp.maximum(check[...], jnp.maximum(most, 1.0 / least))
        mixed = jnp.concatenate(outs, 0).astype(BF16)
        res = x + dot(mixed, proj_ref[block])
        for w in range(count):
            c = dst_cols[w]
            dst[pl.ds(dst_row, 7), c : c + 8, :] = res[56 * w : 56 * w + 56].reshape(
                7, 8, 128
            )

    def feed(block, h):
        y = norm(h, gains_ref[2 + 2 * block : 3 + 2 * block, :] * ROOT_HALF).astype(BF16)
        v = dot(y, fc1_ref[block])
        u = (v * (1.0 + lax.erf(v))).astype(BF16)
        return h + dot(u, fc2_ref[block]) * ROOT_HALF

    def blocks(count, groups, block):
        check[...] = jnp.zeros_like(check)
        lax.fori_loop(0, count, lambda a, _: groups(a, False, block), 0)

        @pl.when(jnp.logical_not(jnp.max(check[...]) < LIMIT))
        def _():
            lax.fori_loop(0, count, lambda a, _: groups(a, True, block), 0)

    def groups0(a, exact, block):
        for g in range(0, wins0, 18):
            cols = [5 + 7 * w for w in range(g, min(g + 18, wins0))]
            attend(block, exact, t0, 7 * a + 1, cols, 7 * a + 5, h1, 7 * a, cols)
        return 0

    for copy in copies[1:4]:
        copy.wait()
    blocks(brows // WIN, groups0, 0)
    for copy in copies[4:6]:
        copy.wait()

    span = tcols + 8

    def feed0(i, _):
        r = 3 + 21 * i
        h = h1[pl.ds(r, 21), 8 : 8 + span, :].reshape(21 * span, 128)
        t = feed(0, h)
        h1[pl.ds(r, 21), 8 : 8 + span, :] = t.reshape(21, span, 128)
        return 0

    lax.fori_loop(0, (trows + WIN) // 21, feed0, 0)

    def groups1(a, exact, block):
        for g in range(0, wins1, 18):
            ws = range(g, min(g + 18, wins1))
            from_cols = [8 + 7 * w for w in ws]
            to_cols = [4 + 7 * w for w in ws]
            attend(block, exact, h1, 3 + 7 * a, from_cols, 8 + 7 * a, h2, 7 * a, to_cols)
        return 0

    blocks(trows // WIN + 1, groups1, 1)

    def feed1(i, _):
        r = 14 * i
        h = h2[pl.ds(4 + r, 14), 8 : 8 + tcols, :].reshape(14 * tcols, 128)
        out_ref[pl.ds(r, 14)] = feed(1, h).astype(BF16).reshape(14, tcols, 128)
        return 0

    lax.fori_loop(0, trows // 14, feed1, 0)


def prepare(
    pattern_ref,
    _,
    stem_ref,
    layer0_ref,
    layer1_ref,
    layer2_ref,
    layer3_ref,
    embed_ref,
    table_ref,
    wst_ref,
    wl_ref,
    e2_ref,
    bias_ref,
    across,
):
    zero = jnp.zeros((C, C), F32)
    for layer, taps_ref in enumerate((layer0_ref, layer1_ref, layer2_ref, layer3_ref)):
        blocks = []
        for b in range(3):
            k0, k1, k2 = [taps_ref[0, 0, 3 * a + b].astype(F32) for a in range(3)]
            blocks.append(jnp.concatenate([k1, k2, zero, k0], 1))
            blocks.append(jnp.concatenate([k0, k1, k2, zero], 1))
        wl_ref[layer] = jnp.concatenate(blocks, 0).T.astype(BF16)

    pattern = pattern_ref[0]
    outer = jnp.logical_or(pattern == 0, pattern == 3)
    row = lax.broadcasted_iota(jnp.int32, (32, 16), 0)
    channel = lax.broadcasted_iota(jnp.int32, (32, 16), 1)
    plane = jnp.where(
        channel == 0,
        pattern,
        jnp.where(
            channel == 1,
            jnp.where(outer, 1, 0),
            jnp.where(channel == 2, jnp.where(outer, 2, 3), 3 - pattern),
        ),
    )
    taps = [
        jnp.concatenate([stem_ref[0, t].astype(F32), jnp.zeros((12, C), F32)], 0).astype(BF16)
        for t in range(9)
    ]
    blocks = []
    for b in range(3):
        for p in range(2):
            total = jnp.zeros((32, C), F32)
            for a in range(3):
                spread = ((row == 8 * (a + p) + plane) & (channel < 4)).astype(BF16)
                total = total + dot(spread, taps[3 * a + b])
            blocks.append(total)
    row = lax.broadcasted_iota(jnp.int32, (32, C), 0)
    for p in range(2):
        blocks.append((row == 8 * (1 + p) + 4).astype(F32))
    wst_ref[...] = jnp.concatenate(blocks, 1).astype(BF16)

    embed = embed_ref[...].astype(F32)
    embed = embed - jnp.mean(embed, -1, keepdims=True)
    high = embed.astype(BF16).astype(F32)
    blank = jnp.zeros_like(embed)
    e2_ref[...] = jnp.concatenate(
        [
            jnp.concatenate(pair, 1)
            for part in (high, embed - high)
            for pair in ((part, blank), (blank, part))
        ],
        0,
    ).astype(BF16)

    table = jnp.concatenate([table_ref[0], table_ref[1]], 0) * LOG2E
    table = jnp.concatenate([table, jnp.zeros((8, 256 - table.shape[1]), F32)], 1)
    part0 = table.astype(BF16)
    part1 = (table - part0.astype(F32)).astype(BF16)
    part2 = (table - part0.astype(F32) - part1.astype(F32)).astype(BF16)
    entry = lax.broadcasted_iota(jnp.int32, (table.shape[1], 128), 0)
    spot = lax.broadcasted_iota(jnp.int32, (table.shape[1], 128), 1)
    base = (12 - lax.shift_right_logical(spot, 3)) * 13 + 6 - (spot & 7)
    for c in range(8):
        pick = (entry == base + min(c, 6)).astype(BF16)
        across[c] = dot(part0, pick) + dot(part1, pick) + dot(part2, pick)
    low = lax.broadcasted_iota(jnp.int32, (1, 128), 1) < 64
    for block in range(2):
        for half in range(2):
            at = 4 * block + 2 * half
            g0 = across[:, at, :]
            g1 = across[:, at + 1, :]
            for r in range(7):
                back = (6 - r) * 8
                bias_ref[block, 8 * r : 8 * r + 8, 128 * half : 128 * half + 128] = jnp.where(
                    low, pltpu.roll(g0, (128 - back) % 128, 1), pltpu.roll(g1, (192 - back) % 128, 1)
                )


def prepared(pattern, candidate, stem_bank, layer_bank, embed_weight, rel_table):
    taps = [
        pl.BlockSpec((1, 1, 9, C, C), lambda i, p, c, n=n: (n, c[n + 1], 0, 0, 0))
        for n in range(LAYERS - 1)
    ]
    return pl.pallas_call(
        prepare,
        out_shape=[
            jax.ShapeDtypeStruct((32, 8 * C), BF16),
            jax.ShapeDtypeStruct((LAYERS - 1, 4 * C, 6 * C), BF16),
            jax.ShapeDtypeStruct((4 * C, 2 * D), BF16),
            jax.ShapeDtypeStruct((2, 56, HEADS * 64), F32),
        ],
        grid_spec=pltpu.PrefetchScalarGridSpec(
            num_scalar_prefetch=2,
            grid=(1,),
            in_specs=[pl.BlockSpec((1, 9, 4, C), lambda i, p, c: (c[0], 0, 0, 0))]
            + taps
            + [
                pl.BlockSpec((C, D), lambda i, p, c: (0, 0)),
                pl.BlockSpec((2, 4, 169), lambda i, p, c: (0, 0, 0)),
            ],
            out_specs=[
                pl.BlockSpec((32, 8 * C), lambda i, p, c: (0, 0)),
                pl.BlockSpec((LAYERS - 1, 4 * C, 6 * C), lambda i, p, c: (0, 0, 0)),
                pl.BlockSpec((4 * C, 2 * D), lambda i, p, c: (0, 0)),
                pl.BlockSpec((2, 56, HEADS * 64), lambda i, p, c: (0, 0, 0)),
            ],
            scratch_shapes=[pltpu.VMEM((8, 8, 128), F32)],
        ),
        compiler_params=pltpu.CompilerParams(vmem_limit_bytes=VMEM),
        cost_estimate=pl.CostEstimate(
            flops=100_000_000, bytes_accessed=4_000_000, transcendentals=0
        ),
    )(
        pattern,
        candidate,
        stem_bank.swapaxes(2, 3),
        layer_bank,
        layer_bank,
        layer_bank,
        layer_bank,
        embed_weight,
        rel_table,
    )


def swaps(values, axis):
    size = lax.axis_size(axis)
    even = [(i, i ^ 1) for i in range(size)]
    odd = [(i, ((i + 1) ^ 1) - 1) for i in range(size)]
    odd = [(i, j % size) for i, j in odd]
    return lax.ppermute(values, axis, even), lax.ppermute(values, axis, odd)


def ordered(pair, axis):
    first, second = pair
    is_even = lax.axis_index(axis) % 2 == 0
    return jnp.where(is_even, second, first), jnp.where(is_even, first, second)


def computed(sizes, *arrays):
    trows, tcols = sizes[:2]
    frows, fcols = trows + 2 * RIM, tcols + 2 * RIM + 8
    pairs = frows // 2
    brows = trows + 2 * WIN
    vmem = pl.BlockSpec(memory_space=pltpu.VMEM)
    return pl.pallas_call(
        functools.partial(kernel, *sizes),
        out_shape=jax.ShapeDtypeStruct((trows, tcols, D), BF16),
        in_specs=[pl.BlockSpec(memory_space=pltpu.SMEM)]
        + [vmem] * 6
        + [pl.BlockSpec(memory_space=pl.ANY)] * 6,
        out_specs=vmem,
        scratch_shapes=[
            pltpu.VMEM((LAYERS - 1, 4 * C, 6 * C), BF16),
            pltpu.VMEM((2, D, 3 * D), BF16),
            pltpu.VMEM((2, D, D), BF16),
            pltpu.VMEM((2, 56, HEADS * 64), F32),
            pltpu.VMEM((2, D, 4 * D), BF16),
            pltpu.VMEM((2, 4 * D, D), BF16),
            pltpu.SemaphoreType.DMA((6,)),
            pltpu.VMEM((frows + 6, 8, fcols), F32),
            pltpu.VMEM((pairs + 1, fcols, 128), F32),
            pltpu.VMEM((pairs + 2, fcols, 128), BF16),
            pltpu.VMEM((pairs + 2, fcols, 128), BF16),
            pltpu.VMEM((fcols, 128), F32),
            pltpu.VMEM((frows + 2, fcols + 8, 128), F32),
            pltpu.VMEM((brows + 2, fcols + 8, 128), F32),
            pltpu.VMEM((brows, fcols + 8, 128), F32),
            pltpu.VMEM((trows + WIN, fcols, 128), F32),
            pltpu.VMEM((8, 128), F32),
        ],
        compiler_params=pltpu.CompilerParams(vmem_limit_bytes=40 * 1024 * 1024),
    )(*arrays)


def shards(
    planes,
    pattern,
    candidate,
    stem_bank,
    layer_bank,
    embed_weight,
    norm_gains,
    qkv_weight,
    proj_weight,
    rel_table,
    fc1_weight,
    fc2_weight,
    labels,
):
    trows, tcols = labels.shape
    nrows, ncols = lax.axis_size("row"), lax.axis_size("col")
    own = jnp.concatenate([planes.swapaxes(0, 1), labels.astype(BF16)[:, None]], 1)
    pair = swaps(own, "row")
    ready = prepared(pattern, candidate, stem_bank, layer_bank, embed_weight, rel_table)
    wst, wl, e2, bias = ready
    above, below = ordered(pair, "row")
    tall = jnp.concatenate([above[trows - RIM :], own, below[:RIM]], 0)
    ends = jnp.concatenate([tall[:, :, :RIM], tall[:, :, tcols - RIM :]], 2)
    first, second = swaps(ends, "col")
    place = jnp.stack([lax.axis_index("row"), lax.axis_index("col")]).astype(jnp.int32)

    return computed(
        (trows, tcols, nrows, ncols),
        place,
        tall,
        first,
        second,
        wst,
        e2,
        norm_gains,
        wl,
        qkv_weight,
        proj_weight,
        bias,
        fc1_weight,
        fc2_weight,
    )


def solution(mesh):
    placed = (
        P(None, "row", "col"),
        P(),
        P(),
        P(),
        P(),
        P(),
        P(),
        P(),
        P(),
        P(),
        P(),
        P(),
        P("row", "col"),
    )
    return jax.shard_map(
        shards, mesh=mesh, in_specs=placed, out_specs=P("row", "col", None), check_vma=False
    )
```
